32 devices in a mesh: sec: 4 (over x, core), dev: 8 (over z, y).
Axes of the slice: x: 2, y: 2, z: 4, core: 2. Of those that a mesh axis runs over, the one named last changes fastest.
Arguments:
- queries: bfloat16 [256, 64, 576], P(('sec', 'dev')), may hold values from -6 to 6
- latent_cache: bfloat16 [256, 1024, 576], P(('sec', 'dev')), may hold values from -9 to 9
- cache_length: int32 [256], P(('sec', 'dev')), may hold values from 2 to 1024, as said below
- residual: bfloat16 [256, 7168], P(('sec', 'dev')), may hold values from -9 to 9
- norm_gain: float32 [7168], replicated, may hold values from 0.1 to 1.9
- value_up: bfloat16 [64, 512, 128], P('dev'), may hold values from -4 to 4
- out_weight: bfloat16 [8192, 7168], P('dev'), may hold values from -0.0625 to 0.0625
- gate_weight: bfloat16 [7168, 8192], P(None, 'dev'), may hold values from -0.0625 to 0.0625
- up_weight: bfloat16 [7168, 8192], P(None, 'dev'), may hold values from -0.0625 to 0.0625
- down_weight: bfloat16 [8192, 7168], P('dev'), may hold values from -0.125 to 0.125
- expert_index: int32 [256, 2], P(('sec', 'dev')), may hold values from 0 to 3, all different within a row; in each aligned block of 4 rows (0 to 3, 4 to 7, ...) at most 3 rows name the same one
- gate_level: int32 [256, 2], P(('sec', 'dev')), may hold values from 1 to 4095
Outputs:
- layer_output: bfloat16 [256, 7168], P(('sec', 'dev'))
The draws below stay inside these ranges and needn't reach their ends.
Inputs may be any that keep to these rules, and one draw needn't show every extreme that they name: `expert_index`: each token names 2 different experts. The rows of one device form 2 aligned blocks of 4 rows, and within such a block no expert is named more than 3 times. `cache_length`: some request of the first 3 sections holds exactly 1024 live positions.
All inputs are finite; a program needn't handle non-finite values.
Results may differ from the reference program's by a relative error of at most 0.03.
Values may be sent and summed in bfloat16 or wider, within the bound.
No kernel may reach another device: no remote copies, remote signals or barrier semaphores. Data moves between devices by JAX's collectives and lax.ppermute only.
A program may use at most 192 MiB of HBM per device.

```python
import math
import jax
import jax.numpy as jnp
import numpy as np
from jax import lax

D = 7168
HEADS = 64
LAT = 512
ROPE = 64
VDIM = 128
FF = 2048
EXPERTS = 4
TOPK = 2
CACHE_LEN = 1024
KV = 576
MB_TOK = 4
CAP = 3
TOKENS = 256
ATT_TOKENS = 192
N_DEV = 8


def draw_latent_cache(key, part):
    shape_all = (TOKENS, CACHE_LEN, KV)
    drawn = jnp.clip(jax.random.normal(jax.random.fold_in(key, 1), shape_all, jnp.float32), -4.0, 4.0)
    return drawn.astype(jnp.bfloat16)


def draw_queries(key, part):
    shape_all = (TOKENS, HEADS, KV)
    drawn = jnp.clip(jax.random.normal(jax.random.fold_in(key, 2), shape_all, jnp.float32), -4.0, 4.0)
    return drawn.astype(jnp.bfloat16)


def draw_cache_length(key, part):
    lengths = jax.random.randint(jax.random.fold_in(key, 3), (TOKENS,), 2, CACHE_LEN + 1)
    spot = jax.random.randint(jax.random.fold_in(key, 4), (), 0, ATT_TOKENS)
    return lengths.at[spot].set(CACHE_LEN).astype(jnp.int32)


def draw_residual(key, part):
    drawn = jnp.clip(jax.random.normal(jax.random.fold_in(key, 7), (TOKENS, D), jnp.float32), -4.0, 4.0)
    return drawn.astype(jnp.bfloat16)


def with_ends(values, key, low, top_value):
    longest = values.shape.index(max(values.shape))
    spots = []
    for shift in (0, 1):
        where = [jax.random.randint(jax.random.fold_in(key, axis), (), 0, length) for axis, length in enumerate(values.shape)]
        where[longest] = (where[longest] + shift) % values.shape[longest]
        spots.append(tuple(where))
    return values.at[spots[0]].set(low).at[spots[1]].set(top_value)


def block_scale(own_key, shape, split, low, top_value):
    factor_of, own = 1.0, jax.random.fold_in(own_key, 6)
    for position, parts in split:
        draws = jnp.exp(jax.random.uniform(jax.random.fold_in(own, position), (parts,), jnp.float32, low / len(split), top_value / len(split)))
        factor_of = factor_of * jnp.repeat(draws, shape[position] // parts).reshape([-1 if axis == position else 1 for axis in range(len(shape))])
    return factor_of


def shared_out(stream_key, own, number, rows, count, top, bound, lean):
    ranking = jax.random.permutation(stream_key, count)
    crowded, common = shares(count, rows * top, bound, lean, True), shares(count, rows * top, bound, lean, False)
    places = jnp.arange(count)

    def named(sizes, turn):
        used = int((sizes > 0).sum())
        fixed = max(1, used // 4)
        passed = fixed + (places - fixed + turn * (used - fixed)) % max(1, count - fixed)
        return jnp.zeros((count,), jnp.int32).at[ranking[jnp.where(places < fixed, places, passed)]].set(jnp.asarray(sizes, jnp.int32))

    sizes = jnp.where(number % 4 == 0, named(crowded, number // 4), named(common, number - number // 4 - 1))
    mixed = jax.random.permutation(jax.random.fold_in(own, 3), count)
    giver, taker = mixed[0:count // 2 * 2:2], mixed[1:count // 2 * 2:2]
    room = jnp.minimum(sizes[giver] - 1, bound - sizes[taker]) // 2
    room = jnp.where((giver == ranking[0]) | (taker == ranking[0]) | (sizes[taker] == 0), 0, jnp.maximum(room, 0))
    passed = jax.random.randint(jax.random.fold_in(own, 4), (count // 2,), 0, 1 << 20) % (room + 1)
    sizes = sizes.at[giver].add(-passed).at[taker].add(passed)
    items = jnp.searchsorted(jnp.cumsum(sizes), jnp.arange(rows * top), side="right").astype(jnp.int32)
    listing = items.reshape(top, rows).T
    listing = listing[jax.random.permutation(jax.random.fold_in(own, 1), rows)]
    turn = jax.random.randint(jax.random.fold_in(own, 2), (rows, 1), 0, top)
    return jnp.take_along_axis(listing, (jnp.arange(top)[None, :] + turn) % top, axis=1)


def shares(number_of, total, reach, lean, full):
    loads = [(1 << 20) // math.isqrt(standing ** lean) + 1 for standing in range(1, number_of + 1)]
    largest = reach if full else min(reach, max(-(-total // number_of), total * loads[0] // sum(loads)))
    least = 1 if total - largest >= number_of - 1 else 0
    holding, rest = [largest] + [least] * (number_of - 1), total - largest - least * (number_of - 1)
    while rest > 0:
        movable = [i for i in range(1, number_of) if holding[i] < largest] or [i for i in range(1, number_of) if holding[i] < reach]
        mass, left = sum([loads[i] for i in movable]), rest
        for i in movable:
            more = min(reach - holding[i], max(1, left * loads[i] // mass), rest)
            holding[i] = holding[i] + more
            rest = rest - more
    return np.array(holding)


def gaussian(stream_key, dims, width, bound, split=(), held_as=jnp.bfloat16):
    array = width * jax.random.normal(stream_key, dims, jnp.float32)
    if split:
        array = array * block_scale(stream_key, dims, split, -0.22, 0.18)
    return jnp.clip(array, -bound, bound).astype(held_as)


def setup_inputs(seed: int = 0) -> dict:
    keys = jax.random.split(jax.random.key(seed), 13)
    queries = draw_queries(jax.random.fold_in(keys[12], 71), 0)
    latent_cache = draw_latent_cache(jax.random.fold_in(keys[12], 71), 0)
    cache_length = draw_cache_length(jax.random.fold_in(keys[12], 71), 0)
    residual = draw_residual(jax.random.fold_in(keys[12], 71), 0)
    norm_gain = jnp.clip(1.0 + 0.18 * jax.random.normal(keys[4], (D,), jnp.float32), 0.1, 1.9)
    value_up = gaussian(keys[5], (HEADS, LAT, VDIM), 0.25, 4.0, ((0, 8),))
    out_weight = gaussian(keys[6], (HEADS * VDIM, D), (HEADS * VDIM) ** -0.5, 0.0625, ((0, 8),))
    gate_weight = gaussian(keys[7], (D, EXPERTS * FF), D ** -0.5, 0.0625, ((1, 8),))
    up_weight = gaussian(keys[8], (D, EXPERTS * FF), D ** -0.5, 0.0625, ((1, 8),))
    down_weight = gaussian(keys[9], (EXPERTS * FF, D), FF ** -0.5, 0.125, ((0, 8),))
    expert_index_keys = jax.random.split(jax.random.fold_in(keys[10], 1), TOKENS // MB_TOK)
    expert_index_turns = jax.random.permutation(jax.random.fold_in(keys[10], 3), TOKENS // MB_TOK)
    expert_index = jax.vmap(lambda own, number: shared_out(jax.random.fold_in(keys[10], 2), own, number, MB_TOK, EXPERTS, TOPK, CAP, 2))(expert_index_keys, expert_index_turns).reshape((TOKENS, TOPK))
    gate_level = with_ends(jax.random.randint(keys[11], (TOKENS, TOPK), 1, 4096), jax.random.fold_in(keys[11], 1), 1, 4095).astype(jnp.int32)
    return dict(queries=queries, latent_cache=latent_cache, cache_length=cache_length, residual=residual, norm_gain=norm_gain, value_up=value_up, out_weight=out_weight, gate_weight=gate_weight, up_weight=up_weight, down_weight=down_weight, expert_index=expert_index, gate_level=gate_level)


def reference(queries, latent_cache, cache_length, residual, norm_gain, value_up, out_weight, gate_weight, up_weight, down_weight, expert_index, gate_level):
    active = ATT_TOKENS
    score_scale = (VDIM + ROPE) ** (-0.5)
    positions = jnp.arange(CACHE_LEN, dtype=jnp.int32)
    value_float = value_up.astype(jnp.float32)

    def attend(item):
        query_one, cache_one, length_one = item
        scores = jnp.dot(query_one, cache_one.T, preferred_element_type=jnp.float32) * score_scale
        usable = positions[None, :] < length_one
        masked = jnp.where(usable, scores, -1e+30)
        highest = lax.optimization_barrier(jnp.max(masked, axis=1, keepdims=True))
        expos = jnp.where(usable, jnp.exp(masked - highest), 0.0)
        weights = (expos / lax.optimization_barrier(jnp.sum(expos, axis=1, keepdims=True))).astype(jnp.bfloat16)
        latent_out = jnp.dot(weights, cache_one, preferred_element_type=jnp.float32)[:, :LAT].astype(jnp.bfloat16)
        head_out = jnp.einsum('hc,hcv->hv', latent_out.astype(jnp.float32), value_float).astype(jnp.bfloat16)
        return jnp.dot(head_out.reshape(1, HEADS * VDIM), out_weight, preferred_element_type=jnp.float32)[0]
    attended = lax.map(attend, (queries[:active], latent_cache[:active], cache_length[:active]))
    stream = (residual[:active].astype(jnp.float32) + attended).astype(jnp.bfloat16)
    stream_float = stream.astype(jnp.float32)
    mean_square = lax.optimization_barrier(jnp.mean(stream_float * stream_float, axis=1, keepdims=True))
    normed = (stream_float * lax.rsqrt(mean_square + 1e-06) * norm_gain).astype(jnp.bfloat16)
    levels = gate_level[:active].astype(jnp.float32)
    mix = levels / lax.optimization_barrier(jnp.sum(levels, axis=1, keepdims=True))
    chosen = expert_index[:active]
    slab_count = N_DEV // EXPERTS
    slab_width = FF // slab_count
    moe = jnp.zeros((active, D), jnp.float32)
    for expert in range(EXPERTS):
        gate_hidden = jnp.dot(normed, gate_weight[:, expert * FF:(expert + 1) * FF], preferred_element_type=jnp.float32)
        up_hidden = jnp.dot(normed, up_weight[:, expert * FF:(expert + 1) * FF], preferred_element_type=jnp.float32)
        activated = (jax.nn.silu(gate_hidden) * up_hidden).astype(jnp.bfloat16).reshape(active, slab_count, slab_width)
        down_slabs = down_weight[expert * FF:(expert + 1) * FF].reshape(slab_count, slab_width, D)
        partial_out = jnp.einsum('tsf,sfd->tsd', activated.astype(jnp.float32), down_slabs.astype(jnp.float32)).astype(jnp.bfloat16)
        slab_total = lax.optimization_barrier(jnp.sum(partial_out.astype(jnp.float32), axis=1))
        weight_of = lax.optimization_barrier(jnp.sum(jnp.where(chosen == expert, mix, 0.0), axis=1))
        moe = moe + weight_of[:, None] * slab_total
    result = (stream_float + moe).astype(jnp.bfloat16)
    rest_rows = jnp.zeros((TOKENS - active, D), jnp.bfloat16)
    return jnp.concatenate([result, rest_rows], axis=0)
```

```python
import jax
import jax.numpy as jnp
from jax import lax
from jax.sharding import PartitionSpec as P

EXPERTS = 4
CHUNKS = 2
LANES = 128


def swap(x, by):
    size = lax.axis_size("dev")
    return lax.ppermute(x, "dev", [(i, i ^ by) for i in range(size)])


def sum_scatter(x, rows):
    pairs = lax.axis_size("dev") // 2
    me = lax.axis_index("dev")
    fast, slow = me % 2, me // 2
    blocks = x.reshape(pairs, 2, rows, x.shape[1])
    kept = lax.dynamic_index_in_dim(blocks, fast, 1, False)
    got = swap(lax.dynamic_index_in_dim(blocks, 1 - fast, 1, False), 1)
    paired = (kept.astype(jnp.float32) + got.astype(jnp.float32)).astype(jnp.bfloat16)
    total = lax.dynamic_index_in_dim(paired, slow, 0, False).astype(jnp.float32)
    for by in reversed(range(1, pairs)):
        sent = lax.dynamic_index_in_dim(paired, slow ^ by, 0, False)
        total = total + swap(sent, 2 * by).astype(jnp.float32)
    return total


def gather_rows(x):
    pairs = lax.axis_size("dev") // 2
    column = [x] + [None] * (pairs - 1)
    for by in reversed(range(1, pairs)):
        column[by] = swap(x, 2 * by)
    column = jnp.stack(column, axis=0)
    return jnp.stack([column, swap(column, 1)], axis=0)


def layer_block(
    queries,
    latent_cache,
    cache_length,
    residual,
    norm_gain,
    value_up,
    out_weight,
    gate_weight,
    up_weight,
    down_weight,
    expert_index,
    gate_level,
):
    group_size = lax.axis_size("dev")
    pairs = group_size // 2
    attending = lax.axis_index("sec") < lax.axis_size("sec") - 1
    me = lax.axis_index("dev")
    fast, slow = me % 2, me // 2
    token_count = queries.shape[0]
    latent_width = value_up.shape[1]
    score_scale = (value_up.shape[2] + queries.shape[2] - latent_width) ** (-0.5)
    width = residual.shape[1]
    part = width // CHUNKS

    scores = (
        jnp.einsum("thc,tpc->thp", queries, latent_cache, preferred_element_type=jnp.float32)
        * score_scale
    )
    position = lax.broadcasted_iota(jnp.int32, (1, 1, latent_cache.shape[1]), 2)
    usable = position < cache_length[:, None, None]
    masked = jnp.where(usable, scores, -1e30)
    highest = jnp.max(masked, axis=2, keepdims=True)
    expos = jnp.where(usable, jnp.exp(masked - highest), 0.0)
    weights = (expos / jnp.sum(expos, axis=2, keepdims=True)).astype(jnp.bfloat16)
    latent_out = jnp.einsum(
        "thp,tpc->thc", weights, latent_cache, preferred_element_type=jnp.float32
    )[:, :, :latent_width].astype(jnp.bfloat16)

    by_heads = lax.all_to_all(latent_out, "dev", split_axis=1, concat_axis=0, tiled=True)
    head_out = jnp.einsum(
        "thc,hcv->thv", by_heads, value_up, preferred_element_type=jnp.float32
    ).astype(jnp.bfloat16)
    head_flat = head_out.reshape(head_out.shape[0], -1)
    attended = []
    for i in range(CHUNKS):
        columns = out_weight[:, i * part : (i + 1) * part]
        product = jnp.dot(head_flat, columns, preferred_element_type=jnp.float32)
        attended.append(sum_scatter(product.astype(jnp.bfloat16), token_count))
    attended = jnp.concatenate(attended, axis=1)
    stream = (residual.astype(jnp.float32) + attended).astype(jnp.bfloat16)
    stream_float = stream.astype(jnp.float32)
    mean_square = jnp.mean(stream_float * stream_float, axis=1, keepdims=True)
    normed = (stream_float * lax.rsqrt(mean_square + 1e-06) * norm_gain).astype(jnp.bfloat16)

    levels = gate_level.astype(jnp.float32)
    mix = levels / jnp.sum(levels, axis=1, keepdims=True)
    lane = lax.broadcasted_iota(jnp.int32, (1, 1, LANES), 2)
    mix_of = jnp.sum(
        jnp.where(expert_index[:, :, None] == lane % EXPERTS, mix[:, :, None], 0.0), axis=1
    )
    high = lax.reduce_precision(mix_of, 8, 7)
    mix_row = jnp.where(lane[0] < EXPERTS, high, mix_of - high).astype(jnp.bfloat16)

    rows = []
    for i in range(CHUNKS):
        piece = normed[:, i * part : (i + 1) * part]
        if i == CHUNKS - 1:
            piece = jnp.concatenate([piece, mix_row], axis=1)
        rows.append(gather_rows(piece).reshape(group_size * token_count, -1))
    mix_rows = rows[-1][:, part:].astype(jnp.float32)
    rows[-1] = rows[-1][:, :part]
    rows = jnp.concatenate(rows, axis=1)
    mine = me // (group_size // EXPERTS)
    mix_mine = jnp.sum(
        jnp.where((lane[0] < 2 * EXPERTS) & (lane[0] % EXPERTS == mine), mix_rows, 0.0),
        axis=1,
        keepdims=True,
    )

    gate_hidden = jnp.dot(rows, gate_weight, preferred_element_type=jnp.float32)
    up_hidden = jnp.dot(rows, up_weight, preferred_element_type=jnp.float32)
    activated = (jax.nn.silu(gate_hidden) * up_hidden).astype(jnp.bfloat16)
    order = activated.reshape(2, pairs, token_count, -1)
    mixes = mix_mine.reshape(2, pairs, token_count, 1)
    slow_of = jnp.arange(pairs) ^ slow
    fast_of = jnp.arange(2) ^ fast
    order = jnp.transpose(order[fast_of][:, slow_of], (1, 0, 2, 3)).reshape(rows.shape[0], -1)
    mixes = jnp.transpose(mixes[fast_of][:, slow_of], (1, 0, 2, 3)).reshape(rows.shape[0], 1)
    moe = []
    for i in range(CHUNKS):
        columns = down_weight[:, i * part : (i + 1) * part]
        product = jnp.dot(order, columns, preferred_element_type=jnp.float32) * mixes
        moe.append(sum_scatter(product.astype(jnp.bfloat16), token_count))
    moe = jnp.concatenate(moe, axis=1)
    result = (stream_float + moe).astype(jnp.bfloat16)
    return jnp.where(attending, result, jnp.zeros_like(result))


def solution(mesh):
    placed = (
        P(("sec", "dev"), None, None),
        P(("sec", "dev"), None, None),
        P(("sec", "dev")),
        P(("sec", "dev"), None),
        P(),
        P("dev", None, None),
        P("dev", None),
        P(None, "dev"),
        P(None, "dev"),
        P("dev", None),
        P(("sec", "dev"), None),
        P(("sec", "dev"), None),
    )
    return jax.shard_map(
        layer_block,
        mesh=mesh,
        in_specs=placed,
        out_specs=P(("sec", "dev"), None),
        check_vma=False,
    )
```

```python
import functools

import jax
import jax.numpy as jnp
from jax import lax
from jax.experimental import pallas as pl
from jax.experimental.pallas import tpu as pltpu
from jax.sharding import PartitionSpec as P

EXPERTS = 4
CHUNKS = 2
LANES = 128


def swap(x, by):
    size = lax.axis_size("dev")
    return lax.ppermute(x, "dev", [(i, i ^ by) for i in range(size)])


def sum_scatter(x, slabs):
    while slabs > 1:
        slabs = slabs // 2
        got = swap(x[:, slabs:], slabs)
        x = (x[:, :slabs].astype(jnp.float32) + got.astype(jnp.float32)).astype(jnp.bfloat16)
    step = lax.axis_size("dev") // x.shape[0]
    total = x[0, 0].astype(jnp.float32)
    for by in reversed(range(1, x.shape[0])):
        total = total + swap(x[by, 0], by * step).astype(jnp.float32)
    return total


def gather_rows(x, slabs):
    column = [x] + [None] * (EXPERTS - 1)
    for by in reversed(range(1, EXPERTS)):
        column[by] = swap(x, by * slabs)
    column = jnp.stack(column, axis=0)[:, None]
    by = 1
    while by < slabs:
        column = jnp.concatenate([column, swap(column, by)], axis=1)
        by = by * 2
    return column


def attend_kernel(scale, groups, place_ref, length_ref, query_ref, cache_ref, out_ref):
    step = pl.program_id(0)
    tokens = query_ref.shape[0]
    heads = query_ref.shape[1]
    latent_width = out_ref.shape[2]
    found = []
    for t in range(tokens):
        scores = lax.dot_general(
            query_ref[t],
            cache_ref[t],
            (((1,), (1,)), ((), ())),
            preferred_element_type=jnp.float32,
        )
        position = lax.broadcasted_iota(jnp.int32, scores.shape, 1)
        usable = position < length_ref[step * tokens + t]
        masked = jnp.where(usable, scores * scale, -1e30)
        highest = jnp.max(masked, axis=1, keepdims=True)
        expos = jnp.where(usable, jnp.exp(masked - highest), 0.0)
        total = jnp.sum(expos, axis=1, keepdims=True)
        summed = jnp.dot(
            expos.astype(jnp.bfloat16),
            cache_ref[t, :, :latent_width],
            preferred_element_type=jnp.float32,
        )
        found.append(summed / total)
    each = heads // groups
    for g in range(groups):
        block = jnp.concatenate([one[g * each : (g + 1) * each] for one in found], axis=0)
        out_ref[g ^ place_ref[0]] = block.astype(jnp.bfloat16)


def attend(queries, latent_cache, cache_length, me, groups, latent_width, scale):
    token_count, heads, key_width = queries.shape
    each = heads // groups
    together = max(2, 16 // each)
    rows = together * each
    return pl.pallas_call(
        functools.partial(attend_kernel, scale, groups),
        out_shape=jax.ShapeDtypeStruct((groups, token_count * each, latent_width), jnp.bfloat16),
        grid_spec=pltpu.PrefetchScalarGridSpec(
            num_scalar_prefetch=2,
            grid=(token_count // together,),
            in_specs=[
                pl.BlockSpec((together, heads, key_width), lambda i, *_: (i, 0, 0)),
                pl.BlockSpec(
                    (together, latent_cache.shape[1], key_width), lambda i, *_: (i, 0, 0)
                ),
            ],
            out_specs=pl.BlockSpec((groups, rows, latent_width), lambda i, *_: (0, i, 0)),
        ),
        compiler_params=pltpu.CompilerParams(vmem_limit_bytes=24 * 1024 * 1024),
        cost_estimate=pl.CostEstimate(
            flops=2 * token_count * heads * latent_cache.shape[1] * (key_width + latent_width),
            bytes_accessed=2 * latent_cache.size,
            transcendentals=token_count * heads * latent_cache.shape[1],
        ),
    )(me.reshape(1), cache_length, queries, latent_cache)


def layer_block(
    queries,
    latent_cache,
    cache_length,
    residual,
    norm_gain,
    value_up,
    out_weight,
    gate_weight,
    up_weight,
    down_weight,
    expert_index,
    gate_level,
):
    group_size = lax.axis_size("dev")
    slabs = group_size // EXPERTS
    attending = lax.axis_index("sec") < lax.axis_size("sec") - 1
    me = lax.axis_index("dev")
    token_count = queries.shape[0]
    latent_width = value_up.shape[1]
    score_scale = (value_up.shape[2] + queries.shape[2] - latent_width) ** (-0.5)
    width = residual.shape[1]
    part = width // CHUNKS

    latent_out = attend(
        queries, latent_cache, cache_length, me, group_size, latent_width, score_scale
    )
    arrived = [latent_out[0]] + [None] * (group_size - 1)
    for by in reversed(range(1, group_size)):
        arrived[by] = swap(latent_out[by], by)
    by_heads = jnp.stack(arrived, axis=0).reshape(
        group_size * token_count, value_up.shape[0], latent_width
    )
    head_out = jnp.einsum(
        "thc,hcv->thv", by_heads, value_up, preferred_element_type=jnp.float32
    ).astype(jnp.bfloat16)
    head_flat = head_out.reshape(head_out.shape[0], -1)
    product = jnp.dot(head_flat, out_weight, preferred_element_type=jnp.float32)
    product = product.astype(jnp.bfloat16).reshape(EXPERTS, slabs, token_count, width)
    attended = [
        sum_scatter(product[..., i * part : (i + 1) * part], slabs) for i in range(CHUNKS)
    ]
    attended = jnp.concatenate(attended, axis=1)
    stream = (residual.astype(jnp.float32) + attended).astype(jnp.bfloat16)
    stream_float = stream.astype(jnp.float32)
    mean_square = jnp.mean(stream_float * stream_float, axis=1, keepdims=True)
    normed = (stream_float * lax.rsqrt(mean_square + 1e-06) * norm_gain).astype(jnp.bfloat16)

    levels = gate_level.astype(jnp.float32)
    mix = levels / jnp.sum(levels, axis=1, keepdims=True)
    lane = lax.broadcasted_iota(jnp.int32, (1, 1, LANES), 2)
    mix_of = jnp.sum(
        jnp.where(expert_index[:, :, None] == lane % EXPERTS, mix[:, :, None], 0.0), axis=1
    )
    high = lax.reduce_precision(mix_of, 8, 7)
    mix_row = jnp.where(lane[0] < EXPERTS, high, mix_of - high).astype(jnp.bfloat16)

    rows = []
    for i in range(CHUNKS):
        piece = normed[:, i * part : (i + 1) * part]
        if i == CHUNKS - 1:
            piece = jnp.concatenate([piece, mix_row], axis=1)
        rows.append(gather_rows(piece, slabs).reshape(group_size * token_count, -1))
    mix_rows = rows[-1][:, part:].astype(jnp.float32)
    rows[-1] = rows[-1][:, :part]
    rows = jnp.concatenate(rows, axis=1)
    mine = me // slabs
    mix_mine = jnp.sum(
        jnp.where((lane[0] < 2 * EXPERTS) & (lane[0] % EXPERTS == mine), mix_rows, 0.0),
        axis=1,
        keepdims=True,
    )

    gate_hidden = jnp.dot(rows, gate_weight, preferred_element_type=jnp.float32)
    up_hidden = jnp.dot(rows, up_weight, preferred_element_type=jnp.float32)
    activated = (jax.nn.silu(gate_hidden) * up_hidden).astype(jnp.bfloat16)
    product = jnp.dot(activated, down_weight, preferred_element_type=jnp.float32) * mix_mine
    product = product.astype(jnp.bfloat16).reshape(EXPERTS, slabs, token_count, width)
    moe = [sum_scatter(product[..., i * part : (i + 1) * part], slabs) for i in range(CHUNKS)]
    moe = jnp.concatenate(moe, axis=1)
    result = (stream_float + moe).astype(jnp.bfloat16)
    return jnp.where(attending, result, jnp.zeros_like(result))


def solution(mesh):
    placed = (
        P(("sec", "dev"), None, None),
        P(("sec", "dev"), None, None),
        P(("sec", "dev")),
        P(("sec", "dev"), None),
        P(),
        P("dev", None, None),
        P("dev", None),
        P(None, "dev"),
        P(None, "dev"),
        P("dev", None),
        P(("sec", "dev"), None),
        P(("sec", "dev"), None),
    )
    return jax.shard_map(
        layer_block,
        mesh=mesh,
        in_specs=placed,
        out_specs=P(("sec", "dev"), None),
        check_vma=False,
    )
```

```python
import functools

import jax
import jax.numpy as jnp
from jax import lax
from jax.experimental import pallas as pl
from jax.experimental.pallas import tpu as pltpu
from jax.sharding import PartitionSpec as P

EXPERTS = 4
CHUNKS = 2
LANES = 128


def swap(x, by):
    size = lax.axis_size("dev")
    return lax.ppermute(x, "dev", [(i, i ^ by) for i in range(size)])


def sum_scatter(x, slabs):
    while slabs > 1:
        slabs = slabs // 2
        got = swap(x[:, slabs:], slabs)
        x = (x[:, :slabs].astype(jnp.float32) + got.astype(jnp.float32)).astype(jnp.bfloat16)
    step = lax.axis_size("dev") // x.shape[0]
    total = x[0, 0].astype(jnp.float32)
    for by in reversed(range(1, x.shape[0])):
        total = total + swap(x[by, 0], by * step).astype(jnp.float32)
    return total


def gather_rows(x, slabs):
    column = [x] + [None] * (EXPERTS - 1)
    for by in reversed(range(1, EXPERTS)):
        column[by] = swap(x, by * slabs)
    column = jnp.stack(column, axis=0)[:, None]
    by = 1
    while by < slabs:
        column = jnp.concatenate([column, swap(column, by)], axis=1)
        by = by * 2
    return column


def streamed(x):
    return pltpu.with_memory_space_constraint(x, pltpu.HBM)


def attend_kernel(
    scale,
    groups,
    together,
    place_ref,
    length_ref,
    query_hbm,
    cache_hbm,
    out_ref,
    query_ref,
    cache_ref,
    query_sem,
    cache_sem,
):
    tokens, heads, _ = query_ref.shape
    latent_width = out_ref.shape[2]
    each = heads // groups
    query_copy = pltpu.make_async_copy(query_hbm, query_ref, query_sem)
    query_copy.start()
    copies = []
    for t in range(tokens):
        copy = pltpu.make_async_copy(cache_hbm.at[t], cache_ref.at[t], cache_sem.at[t])
        copy.start()
        copies.append(copy)
    query_copy.wait()

    def scores_of(t):
        copies[t].wait()
        return jnp.dot(query_ref[t], cache_ref[t], preferred_element_type=jnp.float32)

    scores = scores_of(0)
    found = []
    for t in range(tokens):
        later = scores_of(t + 1) if t + 1 < tokens else None
        position = lax.broadcasted_iota(jnp.int32, scores.shape, 1)
        usable = position < length_ref[t]
        masked = jnp.where(usable, scores * scale, -1e30)
        highest = jnp.max(masked, axis=1, keepdims=True)
        expos = jnp.where(usable, jnp.exp(masked - highest), 0.0)
        total = jnp.sum(expos, axis=1, keepdims=True)
        summed = lax.dot_general(
            expos.astype(jnp.bfloat16),
            cache_ref[t, :latent_width],
            (((1,), (1,)), ((), ())),
            preferred_element_type=jnp.float32,
        )
        found.append(summed / total)
        if len(found) == together:
            first = (t + 1 - together) * each
            for g in range(groups):
                block = jnp.concatenate([one[g * each : (g + 1) * each] for one in found], axis=0)
                out_ref[g ^ place_ref[0], first : first + block.shape[0]] = block.astype(
                    jnp.bfloat16
                )
            found = []
        scores = later


def attend(queries, latent_cache, cache_length, me, groups, latent_width, scale):
    token_count, heads, key_width = queries.shape
    length = latent_cache.shape[1]
    each = heads // groups
    together = max(1, 16 // each)
    return pl.pallas_call(
        functools.partial(attend_kernel, scale, groups, together),
        out_shape=jax.ShapeDtypeStruct((groups, token_count * each, latent_width), jnp.bfloat16),
        in_specs=[pl.BlockSpec(memory_space=pltpu.SMEM)] * 2
        + [pl.BlockSpec(memory_space=pl.ANY)] * 2,
        out_specs=pl.BlockSpec(memory_space=pltpu.VMEM),
        scratch_shapes=[
            pltpu.VMEM(queries.shape, queries.dtype),
            pltpu.VMEM((token_count, key_width, length), latent_cache.dtype),
            pltpu.SemaphoreType.DMA,
            pltpu.SemaphoreType.DMA((token_count,)),
        ],
        compiler_params=pltpu.CompilerParams(vmem_limit_bytes=20 * 1024 * 1024),
        cost_estimate=pl.CostEstimate(
            flops=2 * token_count * heads * length * (key_width + latent_width),
            bytes_accessed=2 * latent_cache.size,
            transcendentals=token_count * heads * length,
        ),
    )(
        me.reshape(1), cache_length, streamed(queries), streamed(jnp.swapaxes(latent_cache, 1, 2))
    )


DEPTH = 256


def project_kernel(first, rows_ref, scale_ref, weight_hbm, out_ref, weight_ref, total_ref, sem):
    depth, count = weight_ref.shape
    copies = []
    for i in range(depth // DEPTH):
        part = pl.ds(i * DEPTH, DEPTH)
        copy = pltpu.make_async_copy(
            weight_hbm.at[part, pl.ds(first, count)], weight_ref.at[part], sem.at[i]
        )
        copy.start()
        copies.append(copy)
    for i, copy in enumerate(copies):
        copy.wait()
        part = pl.ds(i * DEPTH, DEPTH)
        product = jnp.dot(
            rows_ref[:, part], weight_ref[part, :], preferred_element_type=jnp.float32
        )
        if i > 0:
            product = product + total_ref[...]
        if i < len(copies) - 1:
            total_ref[...] = product
        else:
            out_ref[...] = (product * scale_ref[...]).astype(out_ref.dtype)


def project(rows, scale, weight, first, count):
    depth = weight.shape[0]
    vmem = pl.BlockSpec(memory_space=pltpu.VMEM)
    return pl.pallas_call(
        functools.partial(project_kernel, first),
        out_shape=jax.ShapeDtypeStruct((rows.shape[0], count), jnp.bfloat16),
        in_specs=[vmem, vmem, pl.BlockSpec(memory_space=pl.ANY)],
        out_specs=vmem,
        scratch_shapes=[
            pltpu.VMEM((depth, count), weight.dtype),
            pltpu.VMEM((rows.shape[0], count), jnp.float32),
            pltpu.SemaphoreType.DMA((depth // DEPTH,)),
        ],
        compiler_params=pltpu.CompilerParams(vmem_limit_bytes=20 * 1024 * 1024),
        cost_estimate=pl.CostEstimate(
            flops=2 * rows.shape[0] * depth * count,
            bytes_accessed=2 * depth * count,
            transcendentals=0,
        ),
    )(rows, scale, streamed(weight))


def hidden_kernel(
    first, rows_ref, gate_hbm, up_hbm, gate_in, up_in, gate_out, up_out, gate_ref, up_ref, sem
):
    count = gate_ref.shape[0]
    copies = []
    for i in range(count // STEP):
        for k, (source, target) in enumerate(((gate_hbm, gate_ref), (up_hbm, up_ref))):
            copy = pltpu.make_async_copy(
                source.at[pl.ds(first + i * STEP, STEP)],
                target.at[pl.ds(i * STEP, STEP)],
                sem.at[k, i],
            )
            copy.start()
            copies.append(copy)
    for i in range(count // STEP):
        part = pl.ds(i * STEP, STEP)
        for k, (weight, before, after) in enumerate(
            ((gate_ref, gate_in, gate_out), (up_ref, up_in, up_out))
        ):
            copies[2 * i + k].wait()
            product = jnp.dot(
                rows_ref[:, part], weight[part, :], preferred_element_type=jnp.float32
            )
            after[...] = product + (before if i == 0 else after)[...]


STEP = 512


def hidden(rows, gate_weight, up_weight, gate, up, first, count):
    width = gate_weight.shape[1]
    shape = (rows.shape[0], width)
    vmem = pl.BlockSpec(memory_space=pltpu.VMEM)
    hbm = pl.BlockSpec(memory_space=pl.ANY)
    return pl.pallas_call(
        functools.partial(hidden_kernel, first),
        out_shape=[jax.ShapeDtypeStruct(shape, jnp.float32)] * 2,
        in_specs=[vmem, hbm, hbm, vmem, vmem],
        out_specs=[vmem] * 2,
        scratch_shapes=[pltpu.VMEM((count, width), gate_weight.dtype)] * 2
        + [pltpu.SemaphoreType.DMA((2, count // STEP))],
        compiler_params=pltpu.CompilerParams(vmem_limit_bytes=24 * 1024 * 1024),
        cost_estimate=pl.CostEstimate(
            flops=4 * rows.shape[0] * width * count,
            bytes_accessed=4 * width * count,
            transcendentals=0,
        ),
    )(rows, streamed(gate_weight), streamed(up_weight), gate, up)


def layer_block(
    queries,
    latent_cache,
    cache_length,
    residual,
    norm_gain,
    value_up,
    out_weight,
    gate_weight,
    up_weight,
    down_weight,
    expert_index,
    gate_level,
):
    group_size = lax.axis_size("dev")
    slabs = group_size // EXPERTS
    attending = lax.axis_index("sec") < lax.axis_size("sec") - 1
    me = lax.axis_index("dev")
    token_count = queries.shape[0]
    latent_width = value_up.shape[1]
    score_scale = (value_up.shape[2] + queries.shape[2] - latent_width) ** (-0.5)
    width = residual.shape[1]
    part = width // CHUNKS

    latent_out = attend(
        queries, latent_cache, cache_length, me, group_size, latent_width, score_scale
    )
    arrived = [latent_out[0]] + [None] * (group_size - 1)
    for by in reversed(range(1, group_size)):
        arrived[by] = swap(latent_out[by], by)
    by_heads = jnp.stack(arrived, axis=0).reshape(
        group_size * token_count, value_up.shape[0], latent_width
    )
    head_out = jnp.einsum(
        "thc,hcv->thv", by_heads, value_up, preferred_element_type=jnp.float32
    ).astype(jnp.bfloat16)
    head_flat = head_out.reshape(head_out.shape[0], -1)
    ones = jnp.ones((head_flat.shape[0], 1), jnp.float32)
    attended = []
    for i in range(CHUNKS):
        product = project(head_flat, ones, out_weight, i * part, part)
        attended.append(sum_scatter(product.reshape(EXPERTS, slabs, token_count, part), slabs))
    attended = jnp.concatenate(attended, axis=1)
    stream = (residual.astype(jnp.float32) + attended).astype(jnp.bfloat16)
    stream_float = stream.astype(jnp.float32)
    mean_square = jnp.mean(stream_float * stream_float, axis=1, keepdims=True)
    normed = (stream_float * lax.rsqrt(mean_square + 1e-06) * norm_gain).astype(jnp.bfloat16)

    levels = gate_level.astype(jnp.float32)
    mix = levels / jnp.sum(levels, axis=1, keepdims=True)
    lane = lax.broadcasted_iota(jnp.int32, (1, 1, LANES), 2)
    mix_of = jnp.sum(
        jnp.where(expert_index[:, :, None] == lane % EXPERTS, mix[:, :, None], 0.0), axis=1
    )
    high = lax.reduce_precision(mix_of, 8, 7)
    mix_row = jnp.where(lane[0] < EXPERTS, high, mix_of - high).astype(jnp.bfloat16)

    rows = []
    for i in range(CHUNKS):
        piece = normed[:, i * part : (i + 1) * part]
        if i == CHUNKS - 1:
            piece = jnp.concatenate([piece, mix_row], axis=1)
        rows.append(gather_rows(piece, slabs).reshape(group_size * token_count, -1))
    mix_rows = rows[-1][:, part:].astype(jnp.float32)
    rows[-1] = rows[-1][:, :part]
    mine = me // slabs
    mix_mine = jnp.sum(
        jnp.where((lane[0] < 2 * EXPERTS) & (lane[0] % EXPERTS == mine), mix_rows, 0.0),
        axis=1,
        keepdims=True,
    )

    gate = up = jnp.zeros((rows[0].shape[0], gate_weight.shape[1]), jnp.float32)
    for i in range(CHUNKS):
        gate, up = hidden(rows[i], gate_weight, up_weight, gate, up, i * part, part)
    activated = (jax.nn.silu(gate) * up).astype(jnp.bfloat16)
    moe = []
    for i in range(CHUNKS):
        product = project(activated, mix_mine, down_weight, i * part, part)
        moe.append(sum_scatter(product.reshape(EXPERTS, slabs, token_count, part), slabs))
    moe = jnp.concatenate(moe, axis=1)
    result = (stream_float + moe).astype(jnp.bfloat16)
    return jnp.where(attending, result, jnp.zeros_like(result))


def solution(mesh):
    placed = (
        P(("sec", "dev"), None, None),
        P(("sec", "dev"), None, None),
        P(("sec", "dev")),
        P(("sec", "dev"), None),
        P(),
        P("dev", None, None),
        P("dev", None),
        P(None, "dev"),
        P(None, "dev"),
        P("dev", None),
        P(("sec", "dev"), None),
        P(("sec", "dev"), None),
    )
    return jax.shard_map(
        layer_block,
        mesh=mesh,
        in_specs=placed,
        out_specs=P(("sec", "dev"), None),
        check_vma=False,
    )
```

```python
import functools

import jax
import jax.numpy as jnp
from jax import lax
from jax.experimental import pallas as pl
from jax.experimental.pallas import tpu as pltpu
from jax.sharding import PartitionSpec as P

EXPERTS = 4
CHUNKS = 2
LANES = 128


def swap(x, by):
    size = lax.axis_size("dev")
    return lax.ppermute(x, "dev", [(i, i ^ by) for i in range(size)])


def sum_scatter(x, slabs):
    while slabs > 1:
        slabs = slabs // 2
        got = swap(x[:, slabs:], slabs)
        x = (x[:, :slabs].astype(jnp.float32) + got.astype(jnp.float32)).astype(jnp.bfloat16)
    step = lax.axis_size("dev") // x.shape[0]
    total = x[0, 0].astype(jnp.float32)
    for by in reversed(range(1, x.shape[0])):
        total = total + swap(x[by, 0], by * step).astype(jnp.float32)
    return total


def exchange(x, earlier):
    if earlier is not None:
        x, _ = lax.optimization_barrier((x, earlier))
    slabs = x.shape[1]
    column = [x[0]] + [None] * (EXPERTS - 1)
    for by in reversed(range(1, EXPERTS)):
        column[by] = swap(x[by], by * slabs)
    column_first = column[EXPERTS - 1]
    column = jnp.stack(column, axis=0)
    both = [column[:, 0]] + [swap(column[:, by], by) for by in range(1, slabs)]
    return jnp.stack(both, axis=1), column_first


def gather_rows(x, slabs):
    column = [x] + [None] * (EXPERTS - 1)
    for by in reversed(range(1, EXPERTS)):
        column[by] = swap(x, by * slabs)
    column = jnp.stack(column, axis=0)[:, None]
    by = 1
    while by < slabs:
        column = jnp.concatenate([column, swap(column, by)], axis=1)
        by = by * 2
    return column


def streamed(x):
    return pltpu.with_memory_space_constraint(x, pltpu.HBM)


ATTEND_WINDOW = 4


def attend_kernel(
    scale,
    groups,
    together,
    first_token,
    place_ref,
    length_ref,
    query_hbm,
    cache_hbm,
    _,
    out_ref,
    query_ref,
    cache_ref,
    query_sem,
    cache_sem,
):
    tokens, heads, _ = query_ref.shape
    latent_width = out_ref.shape[2]
    each = heads // groups
    chosen = pl.ds(first_token, tokens)
    query_copy = pltpu.make_async_copy(query_hbm.at[chosen], query_ref, query_sem)
    query_copy.start()
    copies = [
        pltpu.make_async_copy(cache_hbm.at[first_token + t], cache_ref.at[t], cache_sem.at[t])
        for t in range(tokens)
    ]
    for copy in copies[:ATTEND_WINDOW]:
        copy.start()
    query_copy.wait()

    def scores_of(t):
        copies[t].wait()
        if t + ATTEND_WINDOW < tokens:
            copies[t + ATTEND_WINDOW].start()
        return jnp.dot(query_ref[t], cache_ref[t], preferred_element_type=jnp.float32)

    scores = scores_of(0)
    found = []
    for t in range(tokens):
        later = scores_of(t + 1) if t + 1 < tokens else None
        position = lax.broadcasted_iota(jnp.int32, scores.shape, 1)
        usable = position < length_ref[first_token + t]
        masked = jnp.where(usable, scores * scale, -1e30)
        highest = jnp.max(masked, axis=1, keepdims=True)
        expos = jnp.where(usable, jnp.exp(masked - highest), 0.0)
        total = jnp.sum(expos, axis=1, keepdims=True)
        summed = lax.dot_general(
            expos.astype(jnp.bfloat16),
            cache_ref[t, :latent_width],
            (((1,), (1,)), ((), ())),
            preferred_element_type=jnp.float32,
        )
        found.append(summed / total)
        if len(found) == together:
            first = (t + 1 - together) * each
            for g in range(groups):
                block = jnp.concatenate([one[g * each : (g + 1) * each] for one in found], axis=0)
                out_ref[g ^ place_ref[0], first : first + block.shape[0]] = block.astype(
                    jnp.bfloat16
                )
            found = []
        scores = later


def attend(queries, latent_cache, cache_length, me, groups, latent_width, scale, first, token_count, after):
    _, heads, key_width = queries.shape
    length = latent_cache.shape[1]
    each = heads // groups
    together = max(1, 16 // each)
    return pl.pallas_call(
        functools.partial(attend_kernel, scale, groups, together, first),
        out_shape=jax.ShapeDtypeStruct((groups, token_count * each, latent_width), jnp.bfloat16),
        in_specs=[pl.BlockSpec(memory_space=pltpu.SMEM)] * 2
        + [pl.BlockSpec(memory_space=pl.ANY)] * 3,
        out_specs=pl.BlockSpec(memory_space=pltpu.VMEM),
        scratch_shapes=[
            pltpu.VMEM((token_count, heads, key_width), queries.dtype),
            pltpu.VMEM((token_count, key_width, length), latent_cache.dtype),
            pltpu.SemaphoreType.DMA,
            pltpu.SemaphoreType.DMA((token_count,)),
        ],
        compiler_params=pltpu.CompilerParams(vmem_limit_bytes=20 * 1024 * 1024),
        cost_estimate=pl.CostEstimate(
            flops=2 * token_count * heads * length * (key_width + latent_width),
            bytes_accessed=2 * token_count * key_width * length,
            transcendentals=token_count * heads * length,
        ),
    )(
        me.reshape(1),
        cache_length,
        streamed(queries),
        streamed(jnp.swapaxes(latent_cache, 1, 2)),
        after,
    )


DEPTH = 256
WINDOW = 16


def project_kernel(first, rows_ref, scale_ref, weight_hbm, out_ref, weight_ref, total_ref, sem):
    depth, count = weight_ref.shape
    copies = []
    for i in range(depth // DEPTH):
        part = pl.ds(i * DEPTH, DEPTH)
        copy = pltpu.make_async_copy(
            weight_hbm.at[part, pl.ds(first, count)], weight_ref.at[part], sem.at[i]
        )
        copies.append(copy)
    for copy in copies[:WINDOW]:
        copy.start()
    for i, copy in enumerate(copies):
        copy.wait()
        if i + WINDOW < len(copies):
            copies[i + WINDOW].start()
        part = pl.ds(i * DEPTH, DEPTH)
        product = jnp.dot(
            rows_ref[:, part], weight_ref[part, :], preferred_element_type=jnp.float32
        )
        if i > 0:
            product = product + total_ref[...]
        if i < len(copies) - 1:
            total_ref[...] = product
        else:
            out_ref[...] = (product * scale_ref[...]).astype(out_ref.dtype)


def project(rows, scale, weight, first, count):
    depth = weight.shape[0]
    vmem = pl.BlockSpec(memory_space=pltpu.VMEM)
    return pl.pallas_call(
        functools.partial(project_kernel, first),
        out_shape=jax.ShapeDtypeStruct((rows.shape[0], count), jnp.bfloat16),
        in_specs=[vmem, vmem, pl.BlockSpec(memory_space=pl.ANY)],
        out_specs=vmem,
        scratch_shapes=[
            pltpu.VMEM((depth, count), weight.dtype),
            pltpu.VMEM((rows.shape[0], count), jnp.float32),
            pltpu.SemaphoreType.DMA((depth // DEPTH,)),
        ],
        compiler_params=pltpu.CompilerParams(vmem_limit_bytes=20 * 1024 * 1024),
        cost_estimate=pl.CostEstimate(
            flops=2 * rows.shape[0] * depth * count,
            bytes_accessed=2 * depth * count,
            transcendentals=0,
        ),
    )(rows, scale, streamed(weight))


def hidden_kernel(
    first, rows_ref, gate_hbm, up_hbm, gate_in, up_in, gate_out, up_out, gate_ref, up_ref, sem
):
    count = gate_ref.shape[0]
    copies = []
    for i in range(count // STEP):
        for k, (source, target) in enumerate(((gate_hbm, gate_ref), (up_hbm, up_ref))):
            copy = pltpu.make_async_copy(
                source.at[pl.ds(first + i * STEP, STEP)],
                target.at[pl.ds(i * STEP, STEP)],
                sem.at[k, i],
            )
            copies.append(copy)
    ahead = 2 * HIDDEN_WINDOW
    for copy in copies[:ahead]:
        copy.start()
    for i in range(count // STEP):
        part = pl.ds(i * STEP, STEP)
        for k, (weight, before, after) in enumerate(
            ((gate_ref, gate_in, gate_out), (up_ref, up_in, up_out))
        ):
            copies[2 * i + k].wait()
            if 2 * i + k + ahead < len(copies):
                copies[2 * i + k + ahead].start()
            product = jnp.dot(
                rows_ref[:, part], weight[part, :], preferred_element_type=jnp.float32
            )
            after[...] = product + (before if i == 0 else after)[...]


STEP = 512
HIDDEN_WINDOW = 16


def hidden(rows, gate_weight, up_weight, gate, up, first, count):
    width = gate_weight.shape[1]
    shape = (rows.shape[0], width)
    vmem = pl.BlockSpec(memory_space=pltpu.VMEM)
    hbm = pl.BlockSpec(memory_space=pl.ANY)
    return pl.pallas_call(
        functools.partial(hidden_kernel, first),
        out_shape=[jax.ShapeDtypeStruct(shape, jnp.float32)] * 2,
        in_specs=[vmem, hbm, hbm, vmem, vmem],
        out_specs=[vmem] * 2,
        scratch_shapes=[pltpu.VMEM((count, width), gate_weight.dtype)] * 2
        + [pltpu.SemaphoreType.DMA((2, count // STEP))],
        compiler_params=pltpu.CompilerParams(vmem_limit_bytes=24 * 1024 * 1024),
        cost_estimate=pl.CostEstimate(
            flops=4 * rows.shape[0] * width * count,
            bytes_accessed=4 * width * count,
            transcendentals=0,
        ),
    )(rows, streamed(gate_weight), streamed(up_weight), gate, up)


def layer_block(
    queries,
    latent_cache,
    cache_length,
    residual,
    norm_gain,
    value_up,
    out_weight,
    gate_weight,
    up_weight,
    down_weight,
    expert_index,
    gate_level,
):
    group_size = lax.axis_size("dev")
    slabs = group_size // EXPERTS
    attending = lax.axis_index("sec") < lax.axis_size("sec") - 1
    me = lax.axis_index("dev")
    token_count = queries.shape[0]
    latent_width = value_up.shape[1]
    score_scale = (value_up.shape[2] + queries.shape[2] - latent_width) ** (-0.5)
    width = residual.shape[1]
    part = width // CHUNKS

    each = queries.shape[1] // group_size
    last = max(1, 16 // each)
    parts = [(0, token_count - last), (token_count - last, last)]
    pieces = []
    latent_out, hop = cache_length, None
    for first, count in parts:
        if count == 0:
            continue
        latent_out = attend(
            queries,
            latent_cache,
            cache_length,
            me,
            group_size,
            latent_width,
            score_scale,
            first,
            count,
            latent_out,
        )
        sent = latent_out.reshape(EXPERTS, slabs, count * each, latent_width)
        arrived, hop = exchange(sent, hop)
        pieces.append(arrived.reshape(group_size, count, each, latent_width))
    by_heads = jnp.concatenate(pieces, axis=1).reshape(
        group_size * token_count, each, latent_width
    )
    head_out = jnp.einsum(
        "thc,hcv->thv", by_heads, value_up, preferred_element_type=jnp.float32
    ).astype(jnp.bfloat16)
    head_flat = head_out.reshape(head_out.shape[0], -1)
    ones = jnp.ones((head_flat.shape[0], 1), jnp.float32)
    attended = []
    for i in range(CHUNKS):
        product = project(head_flat, ones, out_weight, i * part, part)
        attended.append(sum_scatter(product.reshape(EXPERTS, slabs, token_count, part), slabs))
    attended = jnp.concatenate(attended, axis=1)
    stream = (residual.astype(jnp.float32) + attended).astype(jnp.bfloat16)
    stream_float = stream.astype(jnp.float32)
    mean_square = jnp.mean(stream_float * stream_float, axis=1, keepdims=True)
    normed = (stream_float * lax.rsqrt(mean_square + 1e-06) * norm_gain).astype(jnp.bfloat16)

    levels = gate_level.astype(jnp.float32)
    mix = levels / jnp.sum(levels, axis=1, keepdims=True)
    lane = lax.broadcasted_iota(jnp.int32, (1, 1, LANES), 2)
    mix_of = jnp.sum(
        jnp.where(expert_index[:, :, None] == lane % EXPERTS, mix[:, :, None], 0.0), axis=1
    )
    high = lax.reduce_precision(mix_of, 8, 7)
    mix_row = jnp.where(lane[0] < EXPERTS, high, mix_of - high).astype(jnp.bfloat16)

    rows = []
    for i in range(CHUNKS):
        piece = normed[:, i * part : (i + 1) * part]
        if i == CHUNKS - 1:
            piece = jnp.concatenate([piece, mix_row], axis=1)
        rows.append(gather_rows(piece, slabs).reshape(group_size * token_count, -1))
    mix_rows = rows[-1][:, part:].astype(jnp.float32)
    rows[-1] = rows[-1][:, :part]
    mine = me // slabs
    mix_mine = jnp.sum(
        jnp.where((lane[0] < 2 * EXPERTS) & (lane[0] % EXPERTS == mine), mix_rows, 0.0),
        axis=1,
        keepdims=True,
    )

    gate = up = jnp.zeros((rows[0].shape[0], gate_weight.shape[1]), jnp.float32)
    for i in range(CHUNKS):
        gate, up = hidden(rows[i], gate_weight, up_weight, gate, up, i * part, part)
    activated = (jax.nn.silu(gate) * up).astype(jnp.bfloat16)
    moe = []
    for i in range(CHUNKS):
        product = project(activated, mix_mine, down_weight, i * part, part)
        moe.append(sum_scatter(product.reshape(EXPERTS, slabs, token_count, part), slabs))
    moe = jnp.concatenate(moe, axis=1)
    result = (stream_float + moe).astype(jnp.bfloat16)
    return jnp.where(attending, result, jnp.zeros_like(result))


def solution(mesh):
    placed = (
        P(("sec", "dev"), None, None),
        P(("sec", "dev"), None, None),
        P(("sec", "dev")),
        P(("sec", "dev"), None),
        P(),
        P("dev", None, None),
        P("dev", None),
        P(None, "dev"),
        P(None, "dev"),
        P("dev", None),
        P(("sec", "dev"), None),
        P(("sec", "dev"), None),
    )
    return jax.shard_map(
        layer_block,
        mesh=mesh,
        in_specs=placed,
        out_specs=P(("sec", "dev"), None),
        check_vma=False,
    )
```

```python
import functools

import jax
import jax.numpy as jnp
from jax import lax
from jax.experimental import pallas as pl
from jax.experimental.pallas import tpu as pltpu
from jax.sharding import PartitionSpec as P

EXPERTS = 4
SUM_SPLIT = ((0, 4096), (4096, None))
GATHER_SPLIT = ((0, 3072), (3072, None))
MOE_SPLIT = ((0, 4096), (4096, None))
HOPS = (2,1,3)
LANES = 128


def swap(x, by):
    size = lax.axis_size("dev")
    return lax.ppermute(x, "dev", [(i, i ^ by) for i in range(size)])


def sum_scatter(x, slabs):
    while slabs > 1:
        slabs = slabs // 2
        got = swap(x[:, slabs:], slabs)
        x = (x[:, :slabs].astype(jnp.float32) + got.astype(jnp.float32)).astype(jnp.bfloat16)
    step = lax.axis_size("dev") // x.shape[0]
    total = x[0, 0].astype(jnp.float32)
    for by in HOPS:
        total = total + swap(x[by, 0], by * step).astype(jnp.float32)
    return total


def exchange(x, earlier):
    if earlier is not None:
        x, _ = lax.optimization_barrier((x, earlier))
    slabs = x.shape[1]
    column = [x[0]] + [None] * (EXPERTS - 1)
    for by in HOPS:
        column[by] = swap(x[by], by * slabs)
    column_first = column[EXPERTS - 1]
    column = jnp.stack(column, axis=0)
    both = [column[:, 0]] + [swap(column[:, by], by) for by in range(1, slabs)]
    return jnp.stack(both, axis=1), column_first


def gather_rows(x, slabs):
    column = [x] + [None] * (EXPERTS - 1)
    for by in HOPS:
        column[by] = swap(x, by * slabs)
    column = jnp.stack(column, axis=0)[:, None]
    by = 1
    while by < slabs:
        column = jnp.concatenate([column, swap(column, by)], axis=1)
        by = by * 2
    return column


def streamed(x):
    return pltpu.with_memory_space_constraint(x, pltpu.HBM)


ATTEND_WINDOW = 4


def attend_kernel(
    scale,
    groups,
    together,
    first_token,
    place_ref,
    length_hbm,
    query_hbm,
    cache_hbm,
    _,
    out_ref,
    length_ref,
    query_ref,
    cache_ref,
    length_sem,
    query_sem,
    cache_sem,
):
    tokens, heads, _ = query_ref.shape
    latent_width = out_ref.shape[2]
    each = heads // groups
    chosen = pl.ds(first_token, tokens)
    query_copy = pltpu.make_async_copy(query_hbm.at[chosen], query_ref, query_sem)
    query_copy.start()
    length_copy = pltpu.make_async_copy(length_hbm, length_ref, length_sem)
    length_copy.start()
    copies = [
        pltpu.make_async_copy(cache_hbm.at[first_token + t], cache_ref.at[t], cache_sem.at[t])
        for t in range(tokens)
    ]
    for copy in copies[:ATTEND_WINDOW]:
        copy.start()
    length_copy.wait()
    query_copy.wait()

    def scores_of(t):
        copies[t].wait()
        if t + ATTEND_WINDOW < tokens:
            copies[t + ATTEND_WINDOW].start()
        return jnp.dot(query_ref[t], cache_ref[t], preferred_element_type=jnp.float32)

    scores = scores_of(0)
    found = []
    for t in range(tokens):
        later = scores_of(t + 1) if t + 1 < tokens else None
        position = lax.broadcasted_iota(jnp.int32, scores.shape, 1)
        usable = position < length_ref[first_token + t]
        masked = jnp.where(usable, scores * scale, -1e30)
        highest = jnp.max(masked, axis=1, keepdims=True)
        expos = jnp.where(usable, jnp.exp(masked - highest), 0.0)
        total = jnp.sum(expos, axis=1, keepdims=True)
        summed = lax.dot_general(
            expos.astype(jnp.bfloat16),
            cache_ref[t, :latent_width],
            (((1,), (1,)), ((), ())),
            preferred_element_type=jnp.float32,
        )
        found.append(summed / total)
        if len(found) == together:
            first = (t + 1 - together) * each
            for g in range(groups):
                block = jnp.concatenate([one[g * each : (g + 1) * each] for one in found], axis=0)
                out_ref[g ^ place_ref[0], first : first + block.shape[0]] = block.astype(
                    jnp.bfloat16
                )
            found = []
        scores = later


def attend(queries, latent_cache, cache_length, me, groups, latent_width, scale, first, token_count, after):
    _, heads, key_width = queries.shape
    length = latent_cache.shape[1]
    each = heads // groups
    together = max(1, 16 // each)
    return pl.pallas_call(
        functools.partial(attend_kernel, scale, groups, together, first),
        out_shape=jax.ShapeDtypeStruct((groups, token_count * each, latent_width), jnp.bfloat16),
        in_specs=[pl.BlockSpec(memory_space=pltpu.SMEM)]
        + [pl.BlockSpec(memory_space=pl.ANY)] * 4,
        out_specs=pl.BlockSpec(memory_space=pltpu.VMEM),
        scratch_shapes=[
            pltpu.SMEM(cache_length.shape, cache_length.dtype),
            pltpu.VMEM((token_count, heads, key_width), queries.dtype),
            pltpu.VMEM((token_count, key_width, length), latent_cache.dtype),
            pltpu.SemaphoreType.DMA,
            pltpu.SemaphoreType.DMA,
            pltpu.SemaphoreType.DMA((token_count,)),
        ],
        compiler_params=pltpu.CompilerParams(vmem_limit_bytes=20 * 1024 * 1024),
        cost_estimate=pl.CostEstimate(
            flops=2 * token_count * heads * length * (key_width + latent_width),
            bytes_accessed=2 * token_count * key_width * length,
            transcendentals=token_count * heads * length,
        ),
    )(
        me.reshape(1),
        streamed(cache_length),
        streamed(queries),
        streamed(jnp.swapaxes(latent_cache, 1, 2)),
        after,
    )


DEPTH = 256
WINDOW = 16


def project_kernel(first, rows_ref, scale_ref, weight_hbm, out_ref, weight_ref, total_ref, sem):
    depth, count = weight_ref.shape
    copies = []
    for i in range(depth // DEPTH):
        part = pl.ds(i * DEPTH, DEPTH)
        copy = pltpu.make_async_copy(
            weight_hbm.at[part, pl.ds(first, count)], weight_ref.at[part], sem.at[i]
        )
        copies.append(copy)
    for copy in copies[:WINDOW]:
        copy.start()
    for i, copy in enumerate(copies):
        copy.wait()
        if i + WINDOW < len(copies):
            copies[i + WINDOW].start()
        part = pl.ds(i * DEPTH, DEPTH)
        product = jnp.dot(
            rows_ref[:, part], weight_ref[part, :], preferred_element_type=jnp.float32
        )
        if i > 0:
            product = product + total_ref[...]
        if i < len(copies) - 1:
            total_ref[...] = product
        else:
            out_ref[...] = (product * scale_ref[...]).astype(out_ref.dtype)


def project(rows, scale, weight, first, count):
    depth = weight.shape[0]
    vmem = pl.BlockSpec(memory_space=pltpu.VMEM)
    return pl.pallas_call(
        functools.partial(project_kernel, first),
        out_shape=jax.ShapeDtypeStruct((rows.shape[0], count), jnp.bfloat16),
        in_specs=[vmem, vmem, pl.BlockSpec(memory_space=pl.ANY)],
        out_specs=vmem,
        scratch_shapes=[
            pltpu.VMEM((depth, count), weight.dtype),
            pltpu.VMEM((rows.shape[0], count), jnp.float32),
            pltpu.SemaphoreType.DMA((depth // DEPTH,)),
        ],
        compiler_params=pltpu.CompilerParams(vmem_limit_bytes=20 * 1024 * 1024),
        cost_estimate=pl.CostEstimate(
            flops=2 * rows.shape[0] * depth * count,
            bytes_accessed=2 * depth * count,
            transcendentals=0,
        ),
    )(rows, scale, streamed(weight))


def hidden_kernel(
    first, rows_ref, gate_hbm, up_hbm, gate_in, up_in, gate_out, up_out, gate_ref, up_ref, sem
):
    count = gate_ref.shape[0]
    copies = []
    for i in range(count // STEP):
        for k, (source, target) in enumerate(((gate_hbm, gate_ref), (up_hbm, up_ref))):
            copy = pltpu.make_async_copy(
                source.at[pl.ds(first + i * STEP, STEP)],
                target.at[pl.ds(i * STEP, STEP)],
                sem.at[k, i],
            )
            copies.append(copy)
    ahead = 2 * HIDDEN_WINDOW
    for copy in copies[:ahead]:
        copy.start()
    for i in range(count // STEP):
        part = pl.ds(i * STEP, STEP)
        for k, (weight, before, after) in enumerate(
            ((gate_ref, gate_in, gate_out), (up_ref, up_in, up_out))
        ):
            copies[2 * i + k].wait()
            if 2 * i + k + ahead < len(copies):
                copies[2 * i + k + ahead].start()
            product = jnp.dot(
                rows_ref[:, part], weight[part, :], preferred_element_type=jnp.float32
            )
            after[...] = product + (before if i == 0 else after)[...]


STEP = 512
HIDDEN_WINDOW = 16


def hidden(rows, gate_weight, up_weight, gate, up, first, count):
    width = gate_weight.shape[1]
    shape = (rows.shape[0], width)
    vmem = pl.BlockSpec(memory_space=pltpu.VMEM)
    hbm = pl.BlockSpec(memory_space=pl.ANY)
    return pl.pallas_call(
        functools.partial(hidden_kernel, first),
        out_shape=[jax.ShapeDtypeStruct(shape, jnp.float32)] * 2,
        in_specs=[vmem, hbm, hbm, vmem, vmem],
        out_specs=[vmem] * 2,
        scratch_shapes=[pltpu.VMEM((count, width), gate_weight.dtype)] * 2
        + [pltpu.SemaphoreType.DMA((2, count // STEP))],
        compiler_params=pltpu.CompilerParams(vmem_limit_bytes=24 * 1024 * 1024),
        cost_estimate=pl.CostEstimate(
            flops=4 * rows.shape[0] * width * count,
            bytes_accessed=4 * width * count,
            transcendentals=0,
        ),
    )(rows, streamed(gate_weight), streamed(up_weight), gate, up)


def layer_block(
    queries,
    latent_cache,
    cache_length,
    residual,
    norm_gain,
    value_up,
    out_weight,
    gate_weight,
    up_weight,
    down_weight,
    expert_index,
    gate_level,
):
    group_size = lax.axis_size("dev")
    slabs = group_size // EXPERTS
    attending = lax.axis_index("sec") < lax.axis_size("sec") - 1
    me = lax.axis_index("dev")
    token_count = queries.shape[0]
    latent_width = value_up.shape[1]
    score_scale = (value_up.shape[2] + queries.shape[2] - latent_width) ** (-0.5)
    width = residual.shape[1]

    each = queries.shape[1] // group_size
    last = max(1, 16 // each)
    parts = [(0, token_count - last), (token_count - last, last)]
    pieces = []
    latent_out, hop = cache_length, None
    for first, count in parts:
        if count == 0:
            continue
        latent_out = attend(
            queries,
            latent_cache,
            cache_length,
            me,
            group_size,
            latent_width,
            score_scale,
            first,
            count,
            latent_out,
        )
        sent = latent_out.reshape(EXPERTS, slabs, count * each, latent_width)
        arrived, hop = exchange(sent, hop)
        pieces.append(arrived.reshape(group_size, count, each, latent_width))
    by_heads = jnp.concatenate(pieces, axis=1).reshape(
        group_size * token_count, each, latent_width
    )
    head_out = jnp.einsum(
        "thc,hcv->thv", by_heads, value_up, preferred_element_type=jnp.float32
    ).astype(jnp.bfloat16)
    head_flat = head_out.reshape(head_out.shape[0], -1)
    ones = jnp.ones((head_flat.shape[0], 1), jnp.float32)
    attended = []
    for first, end in SUM_SPLIT:
        part = (end or width) - first
        product = project(head_flat, ones, out_weight, first, part)
        attended.append(sum_scatter(product.reshape(EXPERTS, slabs, token_count, part), slabs))
    attended = jnp.concatenate(attended, axis=1)
    stream = (residual.astype(jnp.float32) + attended).astype(jnp.bfloat16)
    stream_float = stream.astype(jnp.float32)
    mean_square = jnp.mean(stream_float * stream_float, axis=1, keepdims=True)
    normed = (stream_float * lax.rsqrt(mean_square + 1e-06) * norm_gain).astype(jnp.bfloat16)

    levels = gate_level.astype(jnp.float32)
    mix = levels / jnp.sum(levels, axis=1, keepdims=True)
    lane = lax.broadcasted_iota(jnp.int32, (1, 1, LANES), 2)
    mix_of = jnp.sum(
        jnp.where(expert_index[:, :, None] == lane % EXPERTS, mix[:, :, None], 0.0), axis=1
    )
    high = lax.reduce_precision(mix_of, 8, 7)
    mix_row = jnp.where(lane[0] < EXPERTS, high, mix_of - high).astype(jnp.bfloat16)

    rows = []
    for first, end in GATHER_SPLIT:
        piece = normed[:, first:end]
        if end is None:
            piece = jnp.concatenate([piece, mix_row], axis=1)
        rows.append(gather_rows(piece, slabs).reshape(group_size * token_count, -1))
    mix_rows = rows[-1][:, -LANES:].astype(jnp.float32)
    rows[-1] = rows[-1][:, :-LANES]
    mine = me // slabs
    mix_mine = jnp.sum(
        jnp.where((lane[0] < 2 * EXPERTS) & (lane[0] % EXPERTS == mine), mix_rows, 0.0),
        axis=1,
        keepdims=True,
    )

    gate = up = jnp.zeros((rows[0].shape[0], gate_weight.shape[1]), jnp.float32)
    for (first, _), piece in zip(GATHER_SPLIT, rows):
        gate, up = hidden(piece, gate_weight, up_weight, gate, up, first, piece.shape[1])
    activated = (jax.nn.silu(gate) * up).astype(jnp.bfloat16)
    moe = []
    for first, end in MOE_SPLIT:
        part = (end or width) - first
        product = project(activated, mix_mine, down_weight, first, part)
        moe.append(sum_scatter(product.reshape(EXPERTS, slabs, token_count, part), slabs))
    moe = jnp.concatenate(moe, axis=1)
    result = (stream_float + moe).astype(jnp.bfloat16)
    return jnp.where(attending, result, jnp.zeros_like(result))


def solution(mesh):
    placed = (
        P(("sec", "dev"), None, None),
        P(("sec", "dev"), None, None),
        P(("sec", "dev")),
        P(("sec", "dev"), None),
        P(),
        P("dev", None, None),
        P("dev", None),
        P(None, "dev"),
        P(None, "dev"),
        P("dev", None),
        P(("sec", "dev"), None),
        P(("sec", "dev"), None),
    )
    return jax.shard_map(
        layer_block,
        mesh=mesh,
        in_specs=placed,
        out_specs=P(("sec", "dev"), None),
        check_vma=False,
    )
```

```python
import functools

import jax
import jax.numpy as jnp
from jax import lax
from jax.experimental import pallas as pl
from jax.experimental.pallas import tpu as pltpu
from jax.sharding import PartitionSpec as P

EXPERTS = 4
SUM_SPLIT = ((0, 4096), (4096, None))
GATHER_SPLIT = ((0, 3072), (3072, None))
MOE_SPLIT = ((0, 4096), (4096, None))
HOPS = (2, 1, 3)
LANES = 128


def swap(x, by):
    size = lax.axis_size("dev")
    return lax.ppermute(x, "dev", [(i, i ^ by) for i in range(size)])


def sum_scatter(x, slabs):
    while slabs > 1:
        slabs = slabs // 2
        got = swap(x[:, slabs:], slabs)
        x = (x[:, :slabs].astype(jnp.float32) + got.astype(jnp.float32)).astype(jnp.bfloat16)
    step = lax.axis_size("dev") // x.shape[0]
    total = x[0, 0].astype(jnp.float32)
    for by in HOPS:
        total = total + swap(x[by, 0], by * step).astype(jnp.float32)
    return total


def exchange(x, earlier):
    if earlier is not None:
        x, _ = lax.optimization_barrier((x, earlier))
    slabs = x.shape[1]
    column = [x[0]] + [None] * (EXPERTS - 1)
    for by in HOPS:
        column[by] = swap(x[by], by * slabs)
    column_first = column[EXPERTS - 1]
    column = jnp.stack(column, axis=0)
    both = [column[:, 0]] + [swap(column[:, by], by) for by in range(1, slabs)]
    return jnp.stack(both, axis=1), column_first


def gather_rows(x, slabs):
    column = [x] + [None] * (EXPERTS - 1)
    for by in HOPS:
        column[by] = swap(x, by * slabs)
    column = jnp.stack(column, axis=0)[:, None]
    by = 1
    while by < slabs:
        column = jnp.concatenate([column, swap(column, by)], axis=1)
        by = by * 2
    return column


def streamed(x):
    return pltpu.with_memory_space_constraint(x, pltpu.HBM)


ATTEND_WINDOW = 3


def attend_kernel(
    scale,
    groups,
    together,
    first_token,
    place_ref,
    length_hbm,
    query_hbm,
    cache_hbm,
    _,
    out_ref,
    length_ref,
    query_ref,
    cache_ref,
    length_sem,
    query_sem,
    cache_sem,
):
    tokens, heads, _ = query_ref.shape
    latent_width = out_ref.shape[2]
    each = heads // groups
    chosen = pl.ds(first_token, tokens)
    query_copy = pltpu.make_async_copy(query_hbm.at[chosen], query_ref, query_sem)
    query_copy.start()
    length_copy = pltpu.make_async_copy(length_hbm, length_ref, length_sem)
    length_copy.start()
    copies = [
        pltpu.make_async_copy(cache_hbm.at[first_token + t], cache_ref.at[t], cache_sem.at[t])
        for t in range(tokens)
    ]
    for copy in copies[:ATTEND_WINDOW]:
        copy.start()
    length_copy.wait()
    query_copy.wait()

    def scores_of(t):
        copies[t].wait()
        if t + ATTEND_WINDOW < tokens:
            copies[t + ATTEND_WINDOW].start()
        return jnp.dot(query_ref[t], cache_ref[t], preferred_element_type=jnp.float32)

    scores = scores_of(0)
    found = []
    for t in range(tokens):
        later = scores_of(t + 1) if t + 1 < tokens else None
        position = lax.broadcasted_iota(jnp.int32, scores.shape, 1)
        usable = position < length_ref[first_token + t]
        masked = jnp.where(usable, scores * scale, -1e30)
        highest = jnp.max(masked, axis=1, keepdims=True)
        expos = jnp.where(usable, jnp.exp(masked - highest), 0.0)
        total = jnp.sum(expos, axis=1, keepdims=True)
        summed = lax.dot_general(
            expos.astype(jnp.bfloat16),
            cache_ref[t, :latent_width],
            (((1,), (1,)), ((), ())),
            preferred_element_type=jnp.float32,
        )
        found.append(summed / total)
        if len(found) == together:
            first = (t + 1 - together) * each
            for g in range(groups):
                block = jnp.concatenate([one[g * each : (g + 1) * each] for one in found], axis=0)
                out_ref[g ^ place_ref[0], first : first + block.shape[0]] = block.astype(
                    jnp.bfloat16
                )
            found = []
        scores = later


def attend(queries, latent_cache, cache_length, me, groups, latent_width, scale, first, token_count, after):
    _, heads, key_width = queries.shape
    length = latent_cache.shape[1]
    each = heads // groups
    together = max(1, 16 // each)
    return pl.pallas_call(
        functools.partial(attend_kernel, scale, groups, together, first),
        out_shape=jax.ShapeDtypeStruct((groups, token_count * each, latent_width), jnp.bfloat16),
        in_specs=[pl.BlockSpec(memory_space=pltpu.SMEM)]
        + [pl.BlockSpec(memory_space=pl.ANY)] * 4,
        out_specs=pl.BlockSpec(memory_space=pltpu.VMEM),
        scratch_shapes=[
            pltpu.SMEM(cache_length.shape, cache_length.dtype),
            pltpu.VMEM((token_count, heads, key_width), queries.dtype),
            pltpu.VMEM((token_count, key_width, length), latent_cache.dtype),
            pltpu.SemaphoreType.DMA,
            pltpu.SemaphoreType.DMA,
            pltpu.SemaphoreType.DMA((token_count,)),
        ],
        compiler_params=pltpu.CompilerParams(vmem_limit_bytes=20 * 1024 * 1024),
        cost_estimate=pl.CostEstimate(
            flops=2 * token_count * heads * length * (key_width + latent_width),
            bytes_accessed=2 * token_count * key_width * length,
            transcendentals=token_count * heads * length,
        ),
    )(
        me.reshape(1),
        streamed(cache_length),
        streamed(queries),
        streamed(jnp.swapaxes(latent_cache, 1, 2)),
        after,
    )


DEPTH = 256
WINDOW = 16


def project_kernel(first, rows_ref, scale_ref, weight_hbm, out_ref, weight_ref, total_ref, sem):
    depth, count = weight_ref.shape
    copies = []
    for i in range(depth // DEPTH):
        part = pl.ds(i * DEPTH, DEPTH)
        copy = pltpu.make_async_copy(
            weight_hbm.at[part, pl.ds(first, count)], weight_ref.at[part], sem.at[i]
        )
        copies.append(copy)
    for copy in copies[:WINDOW]:
        copy.start()
    for i, copy in enumerate(copies):
        copy.wait()
        if i + WINDOW < len(copies):
            copies[i + WINDOW].start()
        part = pl.ds(i * DEPTH, DEPTH)
        product = jnp.dot(
            rows_ref[:, part], weight_ref[part, :], preferred_element_type=jnp.float32
        )
        if i > 0:
            product = product + total_ref[...]
        if i < len(copies) - 1:
            total_ref[...] = product
        else:
            out_ref[...] = (product * scale_ref[...]).astype(out_ref.dtype)


def project(rows, scale, weight, first, count):
    depth = weight.shape[0]
    vmem = pl.BlockSpec(memory_space=pltpu.VMEM)
    return pl.pallas_call(
        functools.partial(project_kernel, first),
        out_shape=jax.ShapeDtypeStruct((rows.shape[0], count), jnp.bfloat16),
        in_specs=[vmem, vmem, pl.BlockSpec(memory_space=pl.ANY)],
        out_specs=vmem,
        scratch_shapes=[
            pltpu.VMEM((depth, count), weight.dtype),
            pltpu.VMEM((rows.shape[0], count), jnp.float32),
            pltpu.SemaphoreType.DMA((depth // DEPTH,)),
        ],
        compiler_params=pltpu.CompilerParams(vmem_limit_bytes=20 * 1024 * 1024),
        cost_estimate=pl.CostEstimate(
            flops=2 * rows.shape[0] * depth * count,
            bytes_accessed=2 * depth * count,
            transcendentals=0,
        ),
    )(rows, scale, streamed(weight))


def hidden_kernel(
    first, finish, rows_ref, gate_hbm, up_hbm, gate_in, up_in, *refs
):
    out_refs, (gate_ref, up_ref, sem) = refs[:-3], refs[-3:]
    count = gate_ref.shape[0]
    copies = []
    for i in range(count // STEP):
        for k, (source, target) in enumerate(((gate_hbm, gate_ref), (up_hbm, up_ref))):
            copy = pltpu.make_async_copy(
                source.at[pl.ds(first + i * STEP, STEP)],
                target.at[pl.ds(i * STEP, STEP)],
                sem.at[k, i],
            )
            copies.append(copy)
    for copy in copies:
        copy.start()
    totals = [gate_in[...], up_in[...]]
    for i in range(count // STEP):
        part = pl.ds(i * STEP, STEP)
        for k, weight in enumerate((gate_ref, up_ref)):
            copies[2 * i + k].wait()
            totals[k] += jnp.dot(
                rows_ref[:, part], weight[part, :], preferred_element_type=jnp.float32
            )
    gate, up = totals
    if finish:
        out_refs[0][...] = (gate / (1.0 + jnp.exp(-gate)) * up).astype(out_refs[0].dtype)
    else:
        out_refs[0][...] = gate
        out_refs[1][...] = up


STEP = 512


def hidden(rows, gate_weight, up_weight, gate, up, first, count, finish):
    width = gate_weight.shape[1]
    shape = (rows.shape[0], width)
    vmem = pl.BlockSpec(memory_space=pltpu.VMEM)
    hbm = pl.BlockSpec(memory_space=pl.ANY)
    return pl.pallas_call(
        functools.partial(hidden_kernel, first, finish),
        out_shape=[jax.ShapeDtypeStruct(shape, jnp.bfloat16)]
        if finish
        else [jax.ShapeDtypeStruct(shape, jnp.float32)] * 2,
        in_specs=[vmem, hbm, hbm, vmem, vmem],
        out_specs=[vmem] * (1 if finish else 2),
        scratch_shapes=[pltpu.VMEM((count, width), gate_weight.dtype)] * 2
        + [pltpu.SemaphoreType.DMA((2, count // STEP))],
        compiler_params=pltpu.CompilerParams(vmem_limit_bytes=24 * 1024 * 1024),
        cost_estimate=pl.CostEstimate(
            flops=4 * rows.shape[0] * width * count,
            bytes_accessed=4 * width * count,
            transcendentals=0,
        ),
    )(rows, streamed(gate_weight), streamed(up_weight), gate, up)


def layer_block(
    queries,
    latent_cache,
    cache_length,
    residual,
    norm_gain,
    value_up,
    out_weight,
    gate_weight,
    up_weight,
    down_weight,
    expert_index,
    gate_level,
):
    group_size = lax.axis_size("dev")
    slabs = group_size // EXPERTS
    attending = lax.axis_index("sec") < lax.axis_size("sec") - 1
    me = lax.axis_index("dev")
    token_count = queries.shape[0]
    latent_width = value_up.shape[1]
    score_scale = (value_up.shape[2] + queries.shape[2] - latent_width) ** (-0.5)
    width = residual.shape[1]

    each = queries.shape[1] // group_size
    last = max(1, 16 // each)
    parts = [(0, token_count - last), (token_count - last, last)]
    pieces = []
    latent_out, hop = cache_length, None
    for first, count in parts:
        if count == 0:
            continue
        latent_out = attend(
            queries,
            latent_cache,
            cache_length,
            me,
            group_size,
            latent_width,
            score_scale,
            first,
            count,
            latent_out,
        )
        sent = latent_out.reshape(EXPERTS, slabs, count * each, latent_width)
        arrived, hop = exchange(sent, hop)
        pieces.append(arrived.reshape(group_size, count, each, latent_width))
    by_heads = jnp.concatenate(pieces, axis=1).reshape(
        group_size * token_count, each, latent_width
    )
    head_out = jnp.einsum(
        "thc,hcv->thv", by_heads, value_up, preferred_element_type=jnp.float32
    ).astype(jnp.bfloat16)
    head_flat = head_out.reshape(head_out.shape[0], -1)
    ones = jnp.ones((head_flat.shape[0], 1), jnp.float32)
    attended = []
    for first, end in SUM_SPLIT:
        part = (end or width) - first
        product = project(head_flat, ones, out_weight, first, part)
        attended.append(sum_scatter(product.reshape(EXPERTS, slabs, token_count, part), slabs))
    attended = jnp.concatenate(attended, axis=1)
    stream = (residual.astype(jnp.float32) + attended).astype(jnp.bfloat16)
    stream_float = stream.astype(jnp.float32)
    mean_square = jnp.mean(stream_float * stream_float, axis=1, keepdims=True)
    normed = (stream_float * lax.rsqrt(mean_square + 1e-06) * norm_gain).astype(jnp.bfloat16)

    levels = gate_level.astype(jnp.float32)
    mix = levels / jnp.sum(levels, axis=1, keepdims=True)
    lane = lax.broadcasted_iota(jnp.int32, (1, 1, LANES), 2)
    mix_of = jnp.sum(
        jnp.where(expert_index[:, :, None] == lane % EXPERTS, mix[:, :, None], 0.0), axis=1
    )
    high = lax.reduce_precision(mix_of, 8, 7)
    mix_row = jnp.where(lane[0] < EXPERTS, high, mix_of - high).astype(jnp.bfloat16)

    rows = []
    for first, end in GATHER_SPLIT:
        piece = normed[:, first:end]
        if end is None:
            piece = jnp.concatenate([piece, mix_row], axis=1)
        rows.append(gather_rows(piece, slabs).reshape(group_size * token_count, -1))
    mix_rows = rows[-1][:, -LANES:].astype(jnp.float32)
    rows[-1] = rows[-1][:, :-LANES]
    mine = me // slabs
    mix_mine = jnp.sum(
        jnp.where((lane[0] < 2 * EXPERTS) & (lane[0] % EXPERTS == mine), mix_rows, 0.0),
        axis=1,
        keepdims=True,
    )

    gate = up = jnp.zeros((rows[0].shape[0], gate_weight.shape[1]), jnp.float32)
    for (first, end), piece in zip(GATHER_SPLIT, rows):
        found = hidden(
            piece, gate_weight, up_weight, gate, up, first, piece.shape[1], end is None
        )
        if end is not None:
            gate, up = found
    (activated,) = found
    moe = []
    for first, end in MOE_SPLIT:
        part = (end or width) - first
        product = project(activated, mix_mine, down_weight, first, part)
        moe.append(sum_scatter(product.reshape(EXPERTS, slabs, token_count, part), slabs))
    moe = jnp.concatenate(moe, axis=1)
    result = (stream_float + moe).astype(jnp.bfloat16)
    return jnp.where(attending, result, jnp.zeros_like(result))


def solution(mesh):
    placed = (
        P(("sec", "dev"), None, None),
        P(("sec", "dev"), None, None),
        P(("sec", "dev")),
        P(("sec", "dev"), None),
        P(),
        P("dev", None, None),
        P("dev", None),
        P(None, "dev"),
        P(None, "dev"),
        P("dev", None),
        P(("sec", "dev"), None),
        P(("sec", "dev"), None),
    )
    return jax.shard_map(
        layer_block,
        mesh=mesh,
        in_specs=placed,
        out_specs=P(("sec", "dev"), None),
        check_vma=False,
    )
```

```python
import functools

import jax
import jax.numpy as jnp
from jax import lax
from jax.experimental import pallas as pl
from jax.experimental.pallas import tpu as pltpu
from jax.sharding import PartitionSpec as P

EXPERTS = 4
SUM_SPLIT = ((0, 4096), (4096, None))
GATHER_SPLIT = ((0, 3072), (3072, None))
MOE_SPLIT = ((0, 4096), (4096, None))
HOPS = (2, 1, 3)
LANES = 128


def swap(x, by):
    size = lax.axis_size("dev")
    return lax.ppermute(x, "dev", [(i, i ^ by) for i in range(size)])


def sum_scatter(x, slabs):
    while slabs > 1:
        slabs = slabs // 2
        got = swap(x[:, slabs:], slabs)
        x = (x[:, :slabs].astype(jnp.float32) + got.astype(jnp.float32)).astype(jnp.bfloat16)
    step = lax.axis_size("dev") // x.shape[0]
    total = x[0, 0].astype(jnp.float32)
    for by in HOPS:
        total = total + swap(x[by, 0], by * step).astype(jnp.float32)
    return total


def exchange(x, earlier):
    if earlier is not None:
        x, _ = lax.optimization_barrier((x, earlier))
    slabs = x.shape[1]
    column = [x[0]] + [None] * (EXPERTS - 1)
    for by in HOPS:
        column[by] = swap(x[by], by * slabs)
    column_first = column[EXPERTS - 1]
    column = jnp.stack(column, axis=0)
    both = [column[:, 0]] + [swap(column[:, by], by) for by in range(1, slabs)]
    return jnp.stack(both, axis=1), column_first


def gather_rows(x, slabs):
    column = [x] + [None] * (EXPERTS - 1)
    for by in HOPS:
        column[by] = swap(x, by * slabs)
    column = jnp.stack(column, axis=0)[:, None]
    by = 1
    while by < slabs:
        column = jnp.concatenate([column, swap(column, by)], axis=1)
        by = by * 2
    return column


def streamed(x):
    return pltpu.with_memory_space_constraint(x, pltpu.HBM)


ATTEND_WINDOW = 3


def attend_kernel(
    scale,
    groups,
    together,
    first_token,
    place_ref,
    length_hbm,
    query_hbm,
    cache_hbm,
    _,
    out_ref,
    length_ref,
    query_ref,
    cache_ref,
    length_sem,
    query_sem,
    cache_sem,
):
    tokens, heads, _ = query_ref.shape
    latent_width = out_ref.shape[2]
    each = heads // groups
    chosen = pl.ds(first_token, tokens)
    query_copy = pltpu.make_async_copy(query_hbm.at[chosen], query_ref, query_sem)
    query_copy.start()
    length_copy = pltpu.make_async_copy(length_hbm, length_ref, length_sem)
    length_copy.start()
    copies = [
        pltpu.make_async_copy(cache_hbm.at[first_token + t], cache_ref.at[t], cache_sem.at[t])
        for t in range(tokens)
    ]
    for copy in copies[:ATTEND_WINDOW]:
        copy.start()
    length_copy.wait()
    query_copy.wait()

    def scores_of(t):
        copies[t].wait()
        if t + ATTEND_WINDOW < tokens:
            copies[t + ATTEND_WINDOW].start()
        return jnp.dot(query_ref[t], cache_ref[t], preferred_element_type=jnp.float32)

    scores = scores_of(0)
    found = []
    for t in range(tokens):
        later = scores_of(t + 1) if t + 1 < tokens else None
        position = lax.broadcasted_iota(jnp.int32, scores.shape, 1)
        usable = position < length_ref[first_token + t]
        masked = jnp.where(usable, scores * scale, -1e30)
        highest = jnp.max(masked, axis=1, keepdims=True)
        expos = jnp.where(usable, jnp.exp(masked - highest), 0.0)
        total = jnp.sum(expos, axis=1, keepdims=True)
        summed = lax.dot_general(
            expos.astype(jnp.bfloat16),
            cache_ref[t, :latent_width],
            (((1,), (1,)), ((), ())),
            preferred_element_type=jnp.float32,
        )
        found.append(summed / total)
        if len(found) == together:
            first = (t + 1 - together) * each
            for g in range(groups):
                block = jnp.concatenate([one[g * each : (g + 1) * each] for one in found], axis=0)
                out_ref[g ^ place_ref[0], first : first + block.shape[0]] = block.astype(
                    jnp.bfloat16
                )
            found = []
        scores = later


def attend(queries, latent_cache, cache_length, me, groups, latent_width, scale, first, token_count, after):
    _, heads, key_width = queries.shape
    length = latent_cache.shape[1]
    each = heads // groups
    together = max(1, 16 // each)
    return pl.pallas_call(
        functools.partial(attend_kernel, scale, groups, together, first),
        out_shape=jax.ShapeDtypeStruct((groups, token_count * each, latent_width), jnp.bfloat16),
        in_specs=[pl.BlockSpec(memory_space=pltpu.SMEM)]
        + [pl.BlockSpec(memory_space=pl.ANY)] * 4,
        out_specs=pl.BlockSpec(memory_space=pltpu.VMEM),
        scratch_shapes=[
            pltpu.SMEM(cache_length.shape, cache_length.dtype),
            pltpu.VMEM((token_count, heads, key_width), queries.dtype),
            pltpu.VMEM((token_count, key_width, length), latent_cache.dtype),
            pltpu.SemaphoreType.DMA,
            pltpu.SemaphoreType.DMA,
            pltpu.SemaphoreType.DMA((token_count,)),
        ],
        compiler_params=pltpu.CompilerParams(vmem_limit_bytes=20 * 1024 * 1024),
        cost_estimate=pl.CostEstimate(
            flops=2 * token_count * heads * length * (key_width + latent_width),
            bytes_accessed=2 * token_count * key_width * length,
            transcendentals=token_count * heads * length,
        ),
    )(
        me.reshape(1),
        streamed(cache_length),
        streamed(queries),
        streamed(jnp.swapaxes(latent_cache, 1, 2)),
        after,
    )


DEPTH = 256
WINDOW = 16


def project_kernel(first, rows_ref, scale_ref, weight_hbm, out_ref, weight_ref, total_ref, sem):
    depth, count = weight_ref.shape
    copies = []
    for i in range(depth // DEPTH):
        part = pl.ds(i * DEPTH, DEPTH)
        copy = pltpu.make_async_copy(
            weight_hbm.at[part, pl.ds(first, count)], weight_ref.at[part], sem.at[i]
        )
        copies.append(copy)
    for copy in copies[:WINDOW]:
        copy.start()
    for i, copy in enumerate(copies):
        copy.wait()
        if i + WINDOW < len(copies):
            copies[i + WINDOW].start()
        part = pl.ds(i * DEPTH, DEPTH)
        product = jnp.dot(
            rows_ref[:, part], weight_ref[part, :], preferred_element_type=jnp.float32
        )
        if i > 0:
            product = product + total_ref[...]
        if i < len(copies) - 1:
            total_ref[...] = product
        else:
            out_ref[...] = (product * scale_ref[...]).astype(out_ref.dtype)


def project(rows, scale, weight, first, count):
    depth = weight.shape[0]
    vmem = pl.BlockSpec(memory_space=pltpu.VMEM)
    return pl.pallas_call(
        functools.partial(project_kernel, first),
        out_shape=jax.ShapeDtypeStruct((rows.shape[0], count), jnp.bfloat16),
        in_specs=[vmem, vmem, pl.BlockSpec(memory_space=pl.ANY)],
        out_specs=vmem,
        scratch_shapes=[
            pltpu.VMEM((depth, count), weight.dtype),
            pltpu.VMEM((rows.shape[0], count), jnp.float32),
            pltpu.SemaphoreType.DMA((depth // DEPTH,)),
        ],
        compiler_params=pltpu.CompilerParams(vmem_limit_bytes=20 * 1024 * 1024),
        cost_estimate=pl.CostEstimate(
            flops=2 * rows.shape[0] * depth * count,
            bytes_accessed=2 * depth * count,
            transcendentals=0,
        ),
    )(rows, scale, streamed(weight))


def hidden_kernel(
    first, finish, rows_ref, gate_hbm, up_hbm, gate_in, up_in, *refs
):
    out_refs, (gate_ref, up_ref, sem) = refs[:-3], refs[-3:]
    count = gate_ref.shape[0]
    copies = []
    for i in range(count // STEP):
        for k, (source, target) in enumerate(((gate_hbm, gate_ref), (up_hbm, up_ref))):
            copy = pltpu.make_async_copy(
                source.at[pl.ds(first + i * STEP, STEP)],
                target.at[pl.ds(i * STEP, STEP)],
                sem.at[k, i],
            )
            copies.append(copy)
    for copy in copies:
        copy.start()
    totals = [gate_in[...], up_in[...]]
    for i in range(count // STEP):
        part = pl.ds(i * STEP, STEP)
        for k, weight in enumerate((gate_ref, up_ref)):
            copies[2 * i + k].wait()
            totals[k] += jnp.dot(
                rows_ref[:, part], weight[part, :], preferred_element_type=jnp.float32
            )
    gate, up = totals
    if finish:
        out_refs[0][...] = (gate / (1.0 + jnp.exp(-gate)) * up).astype(out_refs[0].dtype)
    else:
        out_refs[0][...] = gate
        out_refs[1][...] = up


STEP = 512


def hidden(rows, gate_weight, up_weight, gate, up, first, count, finish):
    width = gate_weight.shape[1]
    shape = (rows.shape[0], width)
    vmem = pl.BlockSpec(memory_space=pltpu.VMEM)
    hbm = pl.BlockSpec(memory_space=pl.ANY)
    return pl.pallas_call(
        functools.partial(hidden_kernel, first, finish),
        out_shape=[jax.ShapeDtypeStruct(shape, jnp.bfloat16)]
        if finish
        else [jax.ShapeDtypeStruct(shape, jnp.float32)] * 2,
        in_specs=[vmem, hbm, hbm, vmem, vmem],
        out_specs=[vmem] * (1 if finish else 2),
        scratch_shapes=[pltpu.VMEM((count, width), gate_weight.dtype)] * 2
        + [pltpu.SemaphoreType.DMA((2, count // STEP))],
        compiler_params=pltpu.CompilerParams(vmem_limit_bytes=24 * 1024 * 1024),
        cost_estimate=pl.CostEstimate(
            flops=4 * rows.shape[0] * width * count,
            bytes_accessed=4 * width * count,
            transcendentals=0,
        ),
    )(rows, streamed(gate_weight), streamed(up_weight), gate, up)


def layer_block(
    queries,
    latent_cache,
    cache_length,
    residual,
    norm_gain,
    value_up,
    out_weight,
    gate_weight,
    up_weight,
    down_weight,
    expert_index,
    gate_level,
):
    group_size = lax.axis_size("dev")
    slabs = group_size // EXPERTS
    attending = lax.axis_index("sec") < lax.axis_size("sec") - 1
    me = lax.axis_index("dev")
    token_count = queries.shape[0]
    latent_width = value_up.shape[1]
    score_scale = (value_up.shape[2] + queries.shape[2] - latent_width) ** (-0.5)
    width = residual.shape[1]

    each = queries.shape[1] // group_size
    last = max(1, 16 // each)
    parts = [(0, token_count - last), (token_count - last, last)]
    pieces = []
    latent_out, hop = cache_length, None
    for first, count in parts:
        if count == 0:
            continue
        latent_out = attend(
            queries,
            latent_cache,
            cache_length,
            me,
            group_size,
            latent_width,
            score_scale,
            first,
            count,
            latent_out,
        )
        sent = latent_out.reshape(EXPERTS, slabs, count * each, latent_width)
        arrived, hop = exchange(sent, hop)
        pieces.append(arrived.reshape(group_size, count, each, latent_width))
    by_heads = jnp.concatenate(pieces, axis=1).reshape(
        group_size * token_count, each, latent_width
    )
    head_out = jnp.einsum(
        "thc,hcv->thv", by_heads, value_up, preferred_element_type=jnp.float32
    ).astype(jnp.bfloat16)
    head_flat = head_out.reshape(head_out.shape[0], -1)
    ones = jnp.ones((head_flat.shape[0], 1), jnp.float32)
    attended = []
    for first, end in SUM_SPLIT:
        part = (end or width) - first
        product = project(head_flat, ones, out_weight, first, part)
        attended.append(sum_scatter(product.reshape(EXPERTS, slabs, token_count, part), slabs))
    attended = jnp.concatenate(attended, axis=1)
    stream = (residual.astype(jnp.float32) + attended).astype(jnp.bfloat16)
    stream_float = stream.astype(jnp.float32)
    mean_square = jnp.mean(stream_float * stream_float, axis=1, keepdims=True)
    normed = (stream_float * lax.rsqrt(mean_square + 1e-06) * norm_gain).astype(jnp.bfloat16)

    levels = gate_level.astype(jnp.float32)
    mix = levels / jnp.sum(levels, axis=1, keepdims=True)
    lane = lax.broadcasted_iota(jnp.int32, (1, 1, LANES), 2)
    mix_of = jnp.sum(
        jnp.where(expert_index[:, :, None] == lane % EXPERTS, mix[:, :, None], 0.0), axis=1
    )
    high = lax.reduce_precision(mix_of, 8, 7)
    mix_row = jnp.where(lane[0] < EXPERTS, high, mix_of - high).astype(jnp.bfloat16)

    rows = []
    for first, end in GATHER_SPLIT:
        piece = normed[:, first:end]
        if first == 0:
            piece = jnp.concatenate([piece, mix_row], axis=1)
        rows.append(gather_rows(piece, slabs).reshape(group_size * token_count, -1))
    mix_rows = rows[0][:, -LANES:].astype(jnp.float32)
    rows[0] = rows[0][:, :-LANES]
    mine = me // slabs
    mix_mine = jnp.sum(
        jnp.where((lane[0] < 2 * EXPERTS) & (lane[0] % EXPERTS == mine), mix_rows, 0.0),
        axis=1,
        keepdims=True,
    )

    gate = up = jnp.zeros((rows[0].shape[0], gate_weight.shape[1]), jnp.float32)
    for (first, end), piece in zip(GATHER_SPLIT, rows):
        found = hidden(
            piece, gate_weight, up_weight, gate, up, first, piece.shape[1], end is None
        )
        if end is not None:
            gate, up = found
    (activated,) = found
    moe = []
    for first, end in MOE_SPLIT:
        part = (end or width) - first
        product = project(activated, mix_mine, down_weight, first, part)
        moe.append(sum_scatter(product.reshape(EXPERTS, slabs, token_count, part), slabs))
    moe = jnp.concatenate(moe, axis=1)
    result = (stream_float + moe).astype(jnp.bfloat16)
    return jnp.where(attending, result, jnp.zeros_like(result))


def solution(mesh):
    placed = (
        P(("sec", "dev"), None, None),
        P(("sec", "dev"), None, None),
        P(("sec", "dev")),
        P(("sec", "dev"), None),
        P(),
        P("dev", None, None),
        P("dev", None),
        P(None, "dev"),
        P(None, "dev"),
        P("dev", None),
        P(("sec", "dev"), None),
        P(("sec", "dev"), None),
    )
    return jax.shard_map(
        layer_block,
        mesh=mesh,
        in_specs=placed,
        out_specs=P(("sec", "dev"), None),
        check_vma=False,
    )
```
